256 devices in a mesh: section: 8 (over y, core), ctx: 32 (over x, z).
Axes of the slice: x: 4, y: 4, z: 8, core: 2. Of those that a mesh axis runs over, the one named last changes fastest.
Arguments:
- carried_rows: bfloat16 [8, 4096, 2048], P('section', 'ctx'), may hold values from -2.5 to 2.5
- fresh_rows: bfloat16 [4096, 2048], P('ctx'), may hold values from -2.5 to 2.5
- queries: bfloat16 [8, 4096, 2048], P('section', 'ctx'), may hold values from -60 to 60
- next_grads: bfloat16 [8, 4096, 2048], P('section', 'ctx'), may hold values from -6 to 6
- loss_grads: bfloat16 [4096, 2048], P('ctx'), may hold values from -6 to 6
- projection: bfloat16 [8, 2048, 1024], P('section'), may hold values from -0.125 to 0.125
- norm_gain: float32 [8, 2048], P('section'), may hold values from 0.1 to 1.9
- key_blocks: int32 [8, 32, 8], P('section', 'ctx'), may hold values from 0 to 31, as said below
- key_valid: int32 [8, 32, 8], P('section', 'ctx'), may hold values from 0 to 1, as said below
Outputs:
- layer_out: bfloat16 [8, 4096, 2048], P('section', 'ctx')
- query_gradient: bfloat16 [8, 4096, 2048], P('section', 'ctx')
- input_grads: bfloat16 [8, 4096, 2048], P('section', 'ctx')
The draws below stay inside these ranges and needn't reach their ends.
Inputs may be any that keep to these rules, and one draw needn't show every extreme that they name: `key_blocks`: for query block i: slot 0 lists block i, slots 1 and 2 list blocks i - 1 and i - 2, slots 3 and 4 blocks 0 and 1, slots 5 to 7 distinct blocks from 2 to i - 3; a slot whose key_valid is 0 lists block i. `key_valid`: slot 0 is always 1; slots 1 to 4 are 1 exactly where their block lies before block i and is not also one of slots 1, 2; among slots 5 to 7 the ones are a leading run of at most i - 4.
All inputs are finite; a program needn't handle non-finite values.
Results may differ from the reference program's by a relative error of at most 0.025.
Values may be sent and summed in bfloat16 or wider, within the bound.
No kernel may reach another device: no remote copies, remote signals or barrier semaphores. Data moves between devices by JAX's collectives and lax.ppermute only.
A program may use at most 128 MiB of HBM per device.

```python
import jax
import jax.numpy as jnp
from jax import lax

D = 2048
HEADS = 16
KV_HEADS = 4
HEAD_DIM = 128
BLOCK = 128
SLOTS = 8
BLK_DEV = 1
SECTIONS = 8
NBLK = 32
SEQ = 4096
N_CTX = 32


def block_lists(key):
    rows = jnp.arange(NBLK, dtype=jnp.int32)
    score_key = jax.random.fold_in(key, 11)
    count_key = jax.random.fold_in(key, 23)
    score_matrix = jax.random.randint(score_key, (SECTIONS, NBLK, NBLK), 0, 1 << 20) * NBLK + rows[None, None, :]
    allowed = (rows[None, :] >= 2) & (rows[None, :] <= rows[:, None] - 3)
    score_matrix = jnp.where(allowed[None, :, :], score_matrix, (1 << 30) + rows[None, None, :])
    picked = jnp.argsort(score_matrix, axis=-1)[..., :3].astype(jnp.int32)
    available = jnp.maximum(rows - 4, 0)
    wanted = jax.random.randint(count_key, (SECTIONS, NBLK), 1, 4)
    count = jnp.minimum(wanted, available[None, :])
    fixed = jnp.stack([rows, rows - 1, rows - 2, jnp.zeros_like(rows), jnp.ones_like(rows)], axis=-1)
    fixed_valid = jnp.stack([rows >= 0, rows >= 1, rows >= 2, rows >= 3, rows >= 4], axis=-1)
    blocks = jnp.concatenate([jnp.broadcast_to(fixed[None], (SECTIONS, NBLK, 5)), picked], axis=-1)
    random_valid = jnp.arange(3, dtype=jnp.int32)[None, None, :] < count[..., None]
    valid = jnp.concatenate([jnp.broadcast_to(fixed_valid[None], (SECTIONS, NBLK, 5)), random_valid], axis=-1)
    blocks = jnp.where(valid, blocks, rows[None, :, None])
    return (blocks.astype(jnp.int32), valid.astype(jnp.int32))


def draw_key_blocks(key, part):
    blocks, valid = block_lists(jax.random.fold_in(key, 5))
    return blocks


def draw_key_valid(key, part):
    blocks, valid = block_lists(jax.random.fold_in(key, 5))
    return valid


def draw_queries(key, part):
    shape = (SECTIONS, SEQ, D)
    value_matrix = jnp.clip(1.5 * jax.random.normal(key, shape, jnp.float32), -9.0, 9.0)
    return value_matrix.astype(jnp.bfloat16)


def shard_levels(own_key, shape, cuts, smallest, largest):
    level, own = 1.0, jax.random.fold_in(own_key, 6)
    for axis_at, shards_of in cuts:
        steps = jnp.exp(jax.random.uniform(jax.random.fold_in(own, axis_at), (shards_of,), jnp.float32, smallest / len(cuts), largest / len(cuts)))
        level = level * jnp.repeat(steps, shape[axis_at] // shards_of).reshape([-1 if axis == axis_at else 1 for axis in range(len(shape))])
    return level


def normal_values(own_key, dims, spread, bound, split=(), kind=jnp.bfloat16):
    result = jax.random.normal(own_key, dims, jnp.float32) * spread
    if len(split) > 0:
        result = shard_levels(own_key, dims, split, -0.22, 0.18) * result
    return jnp.clip(result, min=-bound, max=bound).astype(kind)


def setup_inputs(seed: int = 0) -> dict:
    streams_of = jax.random.split(jax.random.key(seed), 10)
    carried_rows = normal_values(streams_of[0], (SECTIONS, SEQ, D), 0.3, 2.5, ((0, 8), (1, 32)))
    fresh_rows = normal_values(streams_of[1], (SEQ, D), 0.3, 2.5, ((0, 32),))
    queries = draw_queries(jax.random.fold_in(streams_of[9], 71), 0)
    next_grads = normal_values(streams_of[3], (SECTIONS, SEQ, D), 1.0, 6.0, ((0, 8), (1, 32)))
    loss_grads = normal_values(streams_of[4], (SEQ, D), 1.0, 6.0, ((0, 32),))
    projection = normal_values(streams_of[5], (SECTIONS, D, 2 * KV_HEADS * HEAD_DIM), D ** -0.5, 0.125, ((0, 8),))
    norm_gain = jnp.clip(1.0 + 0.18 * jax.random.normal(streams_of[6], (SECTIONS, D), jnp.float32), 0.1, 1.9)
    key_blocks = draw_key_blocks(jax.random.fold_in(streams_of[9], 71), 0)
    key_valid = draw_key_valid(jax.random.fold_in(streams_of[9], 71), 0)
    return {"carried_rows": carried_rows, "fresh_rows": fresh_rows, "queries": queries, "next_grads": next_grads, "loss_grads": loss_grads, "projection": projection, "norm_gain": norm_gain, "key_blocks": key_blocks, "key_valid": key_valid}


rope_base = 500000.0
norm_eps = 1e-05
masked_score = -1e+30

def rotation(positions):
    half = HEAD_DIM // 2
    freqs = rope_base ** (-(jnp.arange(half).astype(jnp.float32) * 2.0) / HEAD_DIM)
    angles = positions.astype(jnp.float32)[:, None] * freqs[None, :]
    return (jnp.cos(angles)[:, None, :], jnp.sin(angles)[:, None, :])

def project_rows(rows, gain, weight, positions):
    width = KV_HEADS * HEAD_DIM
    half = HEAD_DIM // 2
    values_f = rows.astype(jnp.float32)
    scale_inv = lax.rsqrt(lax.optimization_barrier(jnp.mean(values_f * values_f, axis=-1, keepdims=True)) + norm_eps)
    normed = (values_f * scale_inv * gain).astype(jnp.bfloat16)
    mixed = jnp.dot(normed, weight, preferred_element_type=jnp.float32)
    key_matrix = mixed[:, :width].reshape(-1, KV_HEADS, HEAD_DIM)
    cosine, sine = rotation(positions)
    first = key_matrix[..., :half]
    second = key_matrix[..., half:]
    turned = jnp.concatenate([first * cosine - second * sine, first * sine + second * cosine], axis=-1)
    return jnp.concatenate([turned.reshape(-1, width), mixed[:, width:]], axis=-1).astype(jnp.bfloat16)

def attend(query_rows, chosen, valid, grad_rows):
    group = HEADS // KV_HEADS
    width = KV_HEADS * HEAD_DIM
    score_scale = HEAD_DIM ** (-0.5)
    query_head_rows = query_rows.reshape(BLOCK, KV_HEADS, group, HEAD_DIM).astype(jnp.float32)
    key_matrix = chosen[:, :width].reshape(-1, KV_HEADS, HEAD_DIM).astype(jnp.float32)
    value_matrix = chosen[:, width:].reshape(-1, KV_HEADS, HEAD_DIM).astype(jnp.float32)
    score_matrix = jnp.einsum('jpef,npf->pejn', query_head_rows, key_matrix) * score_scale
    key_place = jnp.arange(SLOTS * BLOCK, dtype=jnp.int32)
    slot_of = key_place // BLOCK
    inner = key_place % BLOCK
    slot_ok = jnp.repeat(valid, BLOCK) > 0
    causal = (slot_of[None, :] > 0) | (inner[None, :] <= jnp.arange(BLOCK, dtype=jnp.int32)[:, None])
    allowed = slot_ok[None, :] & causal
    score_matrix = jnp.where(allowed, score_matrix, masked_score)
    highest = lax.optimization_barrier(jnp.max(score_matrix, axis=-1, keepdims=True))
    weights = jnp.exp(score_matrix - highest)
    probs = weights / lax.optimization_barrier(jnp.sum(weights, axis=-1, keepdims=True))
    probabilities_bfloat = lax.optimization_barrier(probs.astype(jnp.bfloat16)).astype(jnp.float32)
    attention_output = jnp.einsum('vqke,eva->kvqa', probabilities_bfloat, value_matrix)
    head_gradient = grad_rows.reshape(BLOCK, KV_HEADS, group, HEAD_DIM).astype(jnp.float32)
    value_gradient = jnp.einsum('bhom,obhf->mbf', probabilities_bfloat, head_gradient)
    probability_gradient = jnp.einsum('jpef,npf->pejn', head_gradient, value_matrix)
    delta = lax.optimization_barrier(jnp.sum(probs * probability_gradient, axis=-1, keepdims=True))
    score_gradient = lax.optimization_barrier((probs * (probability_gradient - delta)).astype(jnp.bfloat16)).astype(jnp.float32)
    query_gradient = jnp.einsum('vqke,eva->kvqa', score_gradient, key_matrix) * score_scale
    key_gradient = jnp.einsum('bhom,obhf->mbf', score_gradient, query_head_rows) * score_scale
    terms = jnp.concatenate([key_gradient.reshape(-1, width), value_gradient.reshape(-1, width)], axis=-1)
    return (attention_output.reshape(BLOCK, D), query_gradient.reshape(BLOCK, D), terms)

def reference(carried_rows, fresh_rows, queries, next_grads, loss_grads, projection, norm_gain, key_blocks, key_valid):
    width = KV_HEADS * HEAD_DIM
    half = HEAD_DIM // 2
    positions = jnp.arange(SEQ, dtype=jnp.int32)
    cosine, sine = rotation(positions)
    block_ids = jnp.arange(NBLK, dtype=jnp.int32)
    layer_list = []
    query_list = []
    input_list = []
    for section_index in range(SECTIONS):
        hidden = fresh_rows if section_index == 0 else carried_rows[section_index - 1]
        grad_out = loss_grads if section_index == SECTIONS - 1 else next_grads[section_index + 1]
        weight = projection[section_index]
        gain = norm_gain[section_index]
        section_queries = queries[section_index]
        blocks = key_blocks[section_index]
        valid = key_valid[section_index]
        kv_all = project_rows(hidden, gain, weight, positions).reshape(NBLK, BLOCK, 2 * width)

        def one_block(block_index):
            start = block_index * BLOCK
            query_rows = lax.dynamic_slice_in_dim(section_queries, start, BLOCK, 0)
            grad_rows = lax.dynamic_slice_in_dim(grad_out, start, BLOCK, 0)
            chosen = jnp.take(kv_all, blocks[block_index], axis=0).reshape(SLOTS * BLOCK, 2 * width)
            return attend(query_rows, chosen, valid[block_index], grad_rows)
        attention_output, query_gradient, partial_terms = lax.map(one_block, block_ids)
        flat_terms = partial_terms.reshape(NBLK * SLOTS, BLOCK * 2 * width)
        flat_names = blocks.reshape(-1)

        def add_device(total, device):
            first = device * (BLK_DEV * SLOTS)
            names_dev = lax.dynamic_slice_in_dim(flat_names, first, BLK_DEV * SLOTS, 0)
            terms_dev = lax.dynamic_slice_in_dim(flat_terms, first, BLK_DEV * SLOTS, 0)
            picks = (names_dev[None, :] == block_ids[:, None]).astype(jnp.float32)
            part_total = jnp.dot(picks, terms_dev, precision=lax.Precision.HIGHEST)
            rounded = lax.optimization_barrier(part_total.astype(jnp.bfloat16)).astype(jnp.float32)
            return (total + rounded, device)
        total, ignored = lax.scan(add_device, jnp.zeros((NBLK, BLOCK * 2 * width), jnp.float32), jnp.arange(N_CTX, dtype=jnp.int32))
        key_sum = total.reshape(SEQ, 2 * width)
        key_part = key_sum[:, :width].reshape(-1, KV_HEADS, HEAD_DIM)
        first_half = key_part[..., :half]
        second_half = key_part[..., half:]
        unturned = jnp.concatenate([first_half * cosine + second_half * sine, second_half * cosine - first_half * sine], axis=-1)
        grads_kv = jnp.concatenate([unturned.reshape(-1, width), key_sum[:, width:]], axis=-1).astype(jnp.bfloat16)
        normed_grads = lax.dot_general(grads_kv, weight, (((1,), (1,)), ((), ())), preferred_element_type=jnp.float32)
        values_f = hidden.astype(jnp.float32)
        scale_inv = lax.rsqrt(lax.optimization_barrier(jnp.mean(values_f * values_f, axis=-1, keepdims=True)) + norm_eps)
        scaled = normed_grads * gain
        correction = lax.optimization_barrier(jnp.mean(scaled * values_f, axis=-1, keepdims=True))
        input_grads = grad_out.astype(jnp.float32) + scale_inv * scaled - values_f * (scale_inv * scale_inv * scale_inv) * correction
        layer_out = hidden.astype(jnp.float32) + attention_output.reshape(SEQ, D)
        layer_list.append(layer_out.astype(jnp.bfloat16))
        query_list.append(query_gradient.reshape(SEQ, D).astype(jnp.bfloat16))
        input_list.append(input_grads.astype(jnp.bfloat16))
    return (jnp.stack(layer_list), jnp.stack(query_list), jnp.stack(input_list))
```

```python
import jax
import jax.numpy as jnp
from jax import lax
from jax.experimental import pallas as pl
from jax.experimental.pallas import tpu as pltpu
from jax.sharding import PartitionSpec as P

D = 2048
HEADS = 16
KV_HEADS = 4
HEAD_DIM = 128
BLOCK = 128
SLOTS = 8
GROUP = HEADS // KV_HEADS
WIDE = GROUP * HEAD_DIM
KEYS = SLOTS * BLOCK

NX = 4
NZ = 8
LIST_ROWS = 16

rope_base = 500000.0
norm_eps = 1e-05
masked_score = -1e30
score_scale = HEAD_DIM ** (-0.5)
log2e = 1.4426950408889634

BF = jnp.bfloat16
F32 = jnp.float32


def shift_section(block, distance):
    devices = range(lax.axis_size("section"))
    route = [(i, i + distance) for i in devices if i + distance in devices]
    return lax.ppermute(block, "section", route)


def shift_z(block, distance):
    route = [
        (x * NZ + z, x * NZ + (z + distance) % NZ) for x in range(NX) for z in range(NZ)
    ]
    return lax.ppermute(block, "ctx", route)


def swap_x(pieces):
    groups = [[x * NZ + z for x in range(NX)] for z in range(NZ)]
    return lax.all_to_all(pieces, "ctx", 0, 0, axis_index_groups=groups)


def vmem():
    return pl.BlockSpec(memory_space=pltpu.VMEM)


def smem():
    return pl.BlockSpec(memory_space=pltpu.SMEM)


def hbm():
    return pl.BlockSpec(memory_space=pl.ANY)


def params(mib=48):
    return pltpu.CompilerParams(vmem_limit_bytes=mib * 2**20)


def turn_tables(block):
    half = HEAD_DIM // 2
    freqs = rope_base ** (-(jnp.arange(half).astype(F32) * 2.0) / HEAD_DIM)
    positions = (block * BLOCK + jnp.arange(BLOCK, dtype=jnp.int32)).astype(F32)
    angles = positions[:, None] * freqs[None, :]
    cosine, sine = jnp.cos(angles), jnp.sin(angles)
    return jnp.concatenate([cosine, cosine], -1), jnp.concatenate([-sine, sine], -1)


def turn_heads(read, out_ref):
    for x in range(NX):
        for g in range(GROUP):
            h = x * GROUP + g
            out_ref[x, :HEAD_DIM, g * BLOCK : (g + 1) * BLOCK] = read(h).T


def queries_body(q_ref, list_ref, out_ref):
    turn_heads(lambda h: q_ref[:, h * HEAD_DIM : (h + 1) * HEAD_DIM], out_ref)
    for x in range(NX):
        out_ref[x, HEAD_DIM:, :] = list_ref[...]


def split_queries(rows, lists):
    return pl.pallas_call(
        queries_body,
        out_shape=jax.ShapeDtypeStruct((NX, HEAD_DIM + LIST_ROWS, WIDE), BF),
        in_specs=[vmem(), vmem()],
        out_specs=vmem(),
        compiler_params=params(),
    )(rows, lists)


def grads_body(edge_ref, moved_ref, fixed_ref, out_ref):
    @pl.when(edge_ref[0] == 1)
    def _():
        turn_heads(lambda h: fixed_ref[:, h * HEAD_DIM : (h + 1) * HEAD_DIM], out_ref)

    @pl.when(edge_ref[0] == 0)
    def _():
        turn_heads(lambda h: moved_ref[:, h * HEAD_DIM : (h + 1) * HEAD_DIM], out_ref)


def split_grads(edge, moved, fixed):
    return pl.pallas_call(
        grads_body,
        out_shape=jax.ShapeDtypeStruct((NX, HEAD_DIM, WIDE), BF),
        in_specs=[smem(), vmem(), vmem()],
        out_specs=vmem(),
        compiler_params=params(),
    )(edge, moved, fixed)


def project_body(edge_ref, moved_ref, fixed_ref, gain_ref, wk_ref, wv_ref, cos_ref, sin_ref, out_ref, normed_ref):
    step = pl.program_id(0)

    @pl.when(step == 0)
    def _():
        rows = jnp.where(edge_ref[0] == 1, fixed_ref[...], moved_ref[...]).astype(F32)
        inv = lax.rsqrt(jnp.mean(rows * rows, axis=-1, keepdims=True) + norm_eps)
        normed_ref[...] = (rows * inv * gain_ref[...]).astype(BF)

    normed = normed_ref[...]
    keys = jnp.dot(normed, wk_ref[...], preferred_element_type=F32)
    values = jnp.dot(normed, wv_ref[...], preferred_element_type=F32)
    for h in range(2):
        k = keys[:, h * HEAD_DIM : (h + 1) * HEAD_DIM]
        turned = k * cos_ref[...] + pltpu.roll(k, HEAD_DIM // 2, 1) * sin_ref[...]
        out_ref[h, 0] = turned.astype(BF)
        out_ref[h, 1] = values[:, h * HEAD_DIM : (h + 1) * HEAD_DIM].astype(BF)


def project(edge, moved, fixed, gain, weight, cosine, sine):
    cols = 2 * HEAD_DIM
    whole = lambda shape: pl.BlockSpec(shape, lambda i: (0,) * len(shape))
    return pl.pallas_call(
        project_body,
        grid=(2,),
        out_shape=jax.ShapeDtypeStruct((KV_HEADS, 2, BLOCK, HEAD_DIM), BF),
        in_specs=[
            smem(),
            whole((BLOCK, D)),
            whole((BLOCK, D)),
            whole((1, D)),
            pl.BlockSpec((D, cols), lambda i: (0, i)),
            pl.BlockSpec((D, cols), lambda i: (0, i + 2)),
            whole((BLOCK, HEAD_DIM)),
            whole((BLOCK, HEAD_DIM)),
        ],
        out_specs=pl.BlockSpec((2, 2, BLOCK, HEAD_DIM), lambda i: (i, 0, 0, 0)),
        scratch_shapes=[pltpu.VMEM((BLOCK, D), BF)],
        compiler_params=params(),
    )(edge, moved, fixed, gain, weight, weight, cosine, sine)


def attend_body(*refs):
    place_ref, valid_ref, q_ref, g_ref = refs[:4]
    kv_refs = refs[4 : 4 + NZ + 1]
    o_ref, dq_ref = refs[13:15]
    d_refs = refs[15 : 15 + NZ]
    held, keys_ref, values_ref, total, sems = refs[15 + NZ :]
    b = pl.program_id(0)

    @pl.when(b == 0)
    def _():
        copies = []
        for r in range(NZ):
            if r < 4:
                copies.append(pltpu.make_async_copy(kv_refs[r], held.at[r], sems.at[r]))
            elif r > 4:
                copies.append(pltpu.make_async_copy(kv_refs[r + 1], held.at[r], sems.at[r]))
        half = NX // 2
        copies.append(pltpu.make_async_copy(kv_refs[4], held.at[4, :half], sems.at[4]))
        copies.append(pltpu.make_async_copy(kv_refs[5], held.at[4, half:], sems.at[8]))
        for c in copies:
            c.start()
        total[...] = jnp.zeros_like(total)
        for c in copies:
            c.wait()

    for s in range(SLOTS):
        at = place_ref[b * SLOTS + s]
        keys_ref[s * BLOCK : (s + 1) * BLOCK, :] = held[at // NX, at % NX, 0]
        values_ref[s * BLOCK : (s + 1) * BLOCK, :] = held[at // NX, at % NX, 1]

    keys = keys_ref[...]
    values = values_ref[...]
    q_t = q_ref[0, :HEAD_DIM, :]
    g_t = g_ref[0]
    scores = jnp.dot(keys, q_t, preferred_element_type=F32) * (score_scale * log2e)
    key_row = lax.broadcasted_iota(jnp.int32, (BLOCK, WIDE), 0)
    query_row = lax.broadcasted_iota(jnp.int32, (BLOCK, WIDE), 1) % BLOCK
    parts = [jnp.where(key_row <= query_row, scores[:BLOCK], masked_score)]
    for s in range(1, SLOTS):
        bias = jnp.where(valid_ref[b * SLOTS + s] > 0, 0.0, masked_score).astype(F32)
        parts.append(scores[s * BLOCK : (s + 1) * BLOCK] + bias)
    scores = jnp.concatenate(parts, axis=0)
    highest = jnp.max(scores, axis=0, keepdims=True)
    weights = jnp.exp2(scores - highest)
    inv = 1.0 / jnp.sum(weights, axis=0, keepdims=True)
    weights_b = weights.astype(BF)
    over_rows = (((0,), (0,)), ((), ()))
    over_cols = (((1,), (1,)), ((), ()))
    out_t = lax.dot_general(values, weights_b, over_rows, preferred_element_type=F32) * inv
    o_ref[0] = out_t.astype(BF)
    g_scaled = (g_t.astype(F32) * inv).astype(BF)
    delta = jnp.sum(out_t * g_scaled.astype(F32), axis=0, keepdims=True)
    d_probs = jnp.dot(values, g_scaled, preferred_element_type=F32)
    d_scores = (weights * (d_probs - delta)).astype(BF)
    dq_t = lax.dot_general(keys, d_scores, over_rows, preferred_element_type=F32) * score_scale
    dq_ref[0] = dq_t.astype(BF)
    d_values = lax.dot_general(weights_b, g_scaled, over_cols, preferred_element_type=F32)
    d_keys = lax.dot_general(d_scores, q_t, over_cols, preferred_element_type=F32) * score_scale
    for s in range(SLOTS):
        at = place_ref[b * SLOTS + s]
        total[at // NX, at % NX, 0] += d_keys[s * BLOCK : (s + 1) * BLOCK]
        total[at // NX, at % NX, 1] += d_values[s * BLOCK : (s + 1) * BLOCK]

    @pl.when(b == NX - 1)
    def _():
        for r in range(NZ):
            d_refs[r][...] = total[r].astype(BF)


def attend(place, valid, q_split, g_split, kv_pieces):
    piece = (NX, 2, BLOCK, HEAD_DIM)
    block_of = lambda rows: pl.BlockSpec((1, rows, WIDE), lambda b: (b, 0, 0))
    full = pl.BlockSpec(piece, lambda b: (0, 0, 0, 0))
    return pl.pallas_call(
        attend_body,
        grid=(NX,),
        out_shape=[
            jax.ShapeDtypeStruct((NX, HEAD_DIM, WIDE), BF),
            jax.ShapeDtypeStruct((NX, HEAD_DIM, WIDE), BF),
        ]
        + [jax.ShapeDtypeStruct(piece, BF)] * NZ,
        in_specs=[smem(), smem(), block_of(HEAD_DIM + LIST_ROWS), block_of(HEAD_DIM)]
        + [hbm()] * len(kv_pieces),
        out_specs=[block_of(HEAD_DIM), block_of(HEAD_DIM)] + [full] * NZ,
        scratch_shapes=[
            pltpu.VMEM((NZ,) + piece, BF),
            pltpu.VMEM((KEYS, HEAD_DIM), BF),
            pltpu.VMEM((KEYS, HEAD_DIM), BF),
            pltpu.VMEM((NZ,) + piece, F32),
            pltpu.SemaphoreType.DMA((9,)),
        ],
        compiler_params=params(56),
    )(place, valid, q_split, g_split, *kv_pieces)


def rows_body(edge_ref, moved_ref, fixed_ref, o_ref, dq_ref, layer_ref, query_ref):
    for x in range(NX):
        for g in range(GROUP):
            at = slice((x * GROUP + g) * HEAD_DIM, (x * GROUP + g + 1) * HEAD_DIM)
            lanes = slice(g * BLOCK, (g + 1) * BLOCK)
            rows = jnp.where(edge_ref[0] == 1, fixed_ref[:, at], moved_ref[:, at]).astype(F32)
            layer_ref[:, at] = (rows + o_ref[x, :, lanes].T.astype(F32)).astype(BF)
            query_ref[:, at] = dq_ref[x, :, lanes].T


def to_rows(edge, moved, fixed, o_split, dq_split):
    return pl.pallas_call(
        rows_body,
        out_shape=[jax.ShapeDtypeStruct((BLOCK, D), BF)] * 2,
        in_specs=[smem()] + [vmem()] * 4,
        out_specs=[vmem(), vmem()],
        compiler_params=params(),
    )(edge, moved, fixed, o_split, dq_split)


def sum_body(*refs):
    total = refs[0][...].astype(F32)
    for r in refs[1:-1]:
        total = total + r[...].astype(F32)
    refs[-1][...] = total.astype(BF)


def sum_pieces(pieces):
    return pl.pallas_call(
        sum_body,
        out_shape=jax.ShapeDtypeStruct(pieces[0].shape, BF),
        in_specs=[vmem()] * len(pieces),
        out_specs=vmem(),
        compiler_params=params(),
    )(*pieces)


def finish_body(edges_ref, h_moved, h_fixed, g_moved, g_fixed, d_ref, gain_ref, w_ref, cos_ref, sin_ref, out_ref):
    columns = []
    for h in range(KV_HEADS):
        k = d_ref[h, 0].astype(F32)
        columns.append(
            (k * cos_ref[...] - pltpu.roll(k, HEAD_DIM // 2, 1) * sin_ref[...]).astype(BF)
        )
    for h in range(KV_HEADS):
        columns.append(d_ref[h, 1])
    grads_kv = jnp.concatenate(columns, axis=-1)
    normed = lax.dot_general(
        grads_kv, w_ref[...], (((1,), (1,)), ((), ())), preferred_element_type=F32
    )
    rows = jnp.where(edges_ref[0] == 1, h_fixed[...], h_moved[...]).astype(F32)
    grads = jnp.where(edges_ref[1] == 1, g_fixed[...], g_moved[...]).astype(F32)
    inv = lax.rsqrt(jnp.mean(rows * rows, axis=-1, keepdims=True) + norm_eps)
    scaled = normed * gain_ref[...]
    correction = jnp.mean(scaled * rows, axis=-1, keepdims=True)
    out_ref[...] = (grads + inv * scaled - rows * (inv * inv * inv * correction)).astype(BF)


def finish(edges, h_moved, h_fixed, g_moved, g_fixed, d_own, gain, weight, cosine, sine):
    return pl.pallas_call(
        finish_body,
        out_shape=jax.ShapeDtypeStruct((BLOCK, D), BF),
        in_specs=[smem()] + [vmem()] * 9,
        out_specs=vmem(),
        compiler_params=params(),
    )(edges, h_moved, h_fixed, g_moved, g_fixed, d_own, gain, weight, cosine, sine)


def per_device(
    carried_rows,
    fresh_rows,
    queries,
    next_grads,
    loss_grads,
    projection,
    norm_gain,
    key_blocks,
    key_valid,
):
    section_now = lax.axis_index("section")
    section_last = lax.axis_size("section") - 1
    me = lax.axis_index("ctx")
    my_z = me % NZ
    first = (section_now == 0).astype(jnp.int32).reshape(1)
    last = (section_now == section_last).astype(jnp.int32).reshape(1)
    edges = jnp.concatenate([first, last])
    weight = projection[0]
    gain = norm_gain[0].reshape(1, D)
    cosine, sine = turn_tables(me)

    h_moved = shift_section(carried_rows[0], 1)
    g_moved = shift_section(next_grads[0], -1)

    lists = jnp.concatenate([key_blocks[0], key_valid[0]], axis=0).astype(BF)
    lists = jnp.pad(lists, ((0, LIST_ROWS - 2), (0, WIDE - SLOTS)))
    q_split = swap_x(split_queries(queries[0], lists))
    named = q_split[:, HEAD_DIM, :SLOTS].astype(jnp.int32)
    valid = q_split[:, HEAD_DIM + 1, :SLOTS].astype(jnp.int32)
    place = ((my_z - named % NZ) % NZ) * NX + named // NZ

    kv_own = swap_x(project(first, h_moved, fresh_rows, gain, weight, cosine, sine))
    g_split = swap_x(split_grads(last, g_moved, loss_grads))

    up, down = [kv_own], [kv_own]
    for _ in range(3):
        up.append(shift_z(up[-1], 1))
        down.append(shift_z(down[-1], -1))
    half = NX // 2
    up_half = shift_z(up[3][:half], 1)
    down_half = shift_z(down[3][half:], -1)
    pieces = [up[0], up[1], up[2], up[3], up_half, down_half, down[3], down[2], down[1]]

    outs = attend(place.reshape(-1), valid.reshape(-1), q_split, g_split, pieces)
    o_split, dq_split, partial = outs[0], outs[1], outs[2:]
    arrived = [partial[0]] + [shift_z(partial[r], -r) for r in (4, 3, 5, 2, 6, 1, 7)]
    layer_out, query_gradient = to_rows(
        first, h_moved, fresh_rows, swap_x(o_split), swap_x(dq_split)
    )
    d_own = swap_x(sum_pieces(arrived))
    input_grads = finish(
        edges, h_moved, fresh_rows, g_moved, loss_grads, d_own, gain, weight, cosine, sine
    )
    return layer_out[None], query_gradient[None], input_grads[None]


def solution(mesh):
    placed = (
        P("section", "ctx", None),
        P("ctx", None),
        P("section", "ctx", None),
        P("section", "ctx", None),
        P("ctx", None),
        P("section", None, None),
        P("section", None),
        P("section", "ctx", None),
        P("section", "ctx", None),
    )
    return jax.shard_map(
        per_device,
        mesh=mesh,
        in_specs=placed,
        out_specs=(P("section", "ctx", None), P("section", "ctx", None), P("section", "ctx", None)),
        check_vma=False,
    )
```

```python
import jax
import jax.numpy as jnp
from jax import lax
from jax.experimental import pallas as pl
from jax.experimental.pallas import tpu as pltpu
from jax.sharding import PartitionSpec as P

D = 2048
HEADS = 16
KV_HEADS = 4
HEAD_DIM = 128
BLOCK = 128
SLOTS = 8
GROUP = HEADS // KV_HEADS
WIDE = GROUP * HEAD_DIM
KEYS = SLOTS * BLOCK

NX = 4
NZ = 8
LIST_ROWS = 16
STAGE_PARTS = 8

rope_base = 500000.0
norm_eps = 1e-05
masked_score = -1e30
score_scale = HEAD_DIM ** (-0.5)
log2e = 1.4426950408889634

BF = jnp.bfloat16
F32 = jnp.float32


def shift_section(block, distance):
    devices = range(lax.axis_size("section"))
    route = [(i, i + distance) for i in devices if i + distance in devices]
    return lax.ppermute(block, "section", route)


def shift_z(block, distance):
    route = [
        (x * NZ + z, x * NZ + (z + distance) % NZ) for x in range(NX) for z in range(NZ)
    ]
    return lax.ppermute(block, "ctx", route)


def swap_x(pieces):
    groups = [[x * NZ + z for x in range(NX)] for z in range(NZ)]
    return lax.all_to_all(pieces, "ctx", 0, 0, axis_index_groups=groups)


def shift_x(block, distance):
    route = [
        (x * NZ + z, (x + distance) % NX * NZ + z) for x in range(NX) for z in range(NZ)
    ]
    return lax.ppermute(block, "ctx", route)


def vmem():
    return pl.BlockSpec(memory_space=pltpu.VMEM)


def smem():
    return pl.BlockSpec(memory_space=pltpu.SMEM)


def hbm():
    return pl.BlockSpec(memory_space=pltpu.HBM)


def params(mib=12):
    return pltpu.CompilerParams(vmem_limit_bytes=mib * 2**20)


def turn_tables(block):
    half = HEAD_DIM // 2
    freqs = rope_base ** (-(jnp.arange(half).astype(F32) * 2.0) / HEAD_DIM)
    positions = (block * BLOCK + jnp.arange(BLOCK, dtype=jnp.int32)).astype(F32)
    angles = positions[:, None] * freqs[None, :]
    cosine, sine = jnp.cos(angles), jnp.sin(angles)
    return jnp.concatenate([cosine, cosine], -1), jnp.concatenate([-sine, sine], -1)


def split_body(where_ref, q_ref, moved_ref, fixed_ref, list_ref, *refs):
    dest_refs, out_refs, grads_ref, sems = refs[: NX + 1], refs[NX + 1], refs[NX + 2], refs[NX + 3]

    @pl.when(where_ref[0] == 1)
    def _():
        fetch = pltpu.make_async_copy(fixed_ref, grads_ref, sems.at[0])
        fetch.start()
        fetch.wait()

    @pl.when(where_ref[0] == 0)
    def _():
        grads_ref[...] = moved_ref[...]

    copies = [pltpu.make_async_copy(grads_ref, dest_refs[NX], sems.at[NX])]
    copies[0].start()
    for k in (1, 2, 3, 0):
        x = (where_ref[1] + k) % NX
        for part, rows_ref in enumerate((q_ref, grads_ref)):
            first = part * HEAD_DIM
            for g in range(GROUP):
                at = pl.ds(pl.multiple_of(x * WIDE + g * HEAD_DIM, HEAD_DIM), HEAD_DIM)
                out_refs[k, first : first + HEAD_DIM, g * BLOCK : (g + 1) * BLOCK] = rows_ref[
                    :, at
                ].T
        out_refs[k, 2 * HEAD_DIM :, :] = list_ref[...]
        copies.append(pltpu.make_async_copy(out_refs.at[k], dest_refs[k], sems.at[k]))
        copies[-1].start()
    for c in copies:
        c.wait()


def split_rows(where, rows, moved, fixed, lists):
    return pl.pallas_call(
        split_body,
        out_shape=[jax.ShapeDtypeStruct((2 * HEAD_DIM + LIST_ROWS, WIDE), BF)] * NX
        + [jax.ShapeDtypeStruct((BLOCK, D), BF)],
        in_specs=[smem(), vmem(), vmem(), hbm(), vmem()],
        out_specs=[hbm()] * (NX + 1),
        scratch_shapes=[
            pltpu.VMEM((NX, 2 * HEAD_DIM + LIST_ROWS, WIDE), BF),
            pltpu.VMEM((BLOCK, D), BF),
            pltpu.SemaphoreType.DMA((NX + 1,)),
        ],
        compiler_params=params(),
    )(where, rows, moved, fixed, lists)


def stage_body(w_ref, gain_ref, w_out, gain_out, sems):
    part = D // STAGE_PARTS
    copies = [
        pltpu.make_async_copy(
            w_ref.at[0, p * part : (p + 1) * part, :],
            w_out.at[p * part : (p + 1) * part, :],
            sems.at[p],
        )
        for p in range(STAGE_PARTS)
    ]
    copies.append(pltpu.make_async_copy(gain_ref, gain_out, sems.at[STAGE_PARTS]))
    for c in copies:
        c.start()
    for c in copies:
        c.wait()


def stage(weight, gain):
    return pl.pallas_call(
        stage_body,
        out_shape=[
            jax.ShapeDtypeStruct(weight.shape[1:], BF),
            jax.ShapeDtypeStruct(gain.shape, F32),
        ],
        in_specs=[hbm(), hbm()],
        out_specs=[vmem(), vmem()],
        scratch_shapes=[pltpu.SemaphoreType.DMA((STAGE_PARTS + 1,))],
        compiler_params=params(8),
    )(weight, gain)


def project_body(edge_ref, moved_ref, fixed_ref, gain_ref, w_ref, cos_ref, sin_ref, out_ref, hidden_ref, rows_ref, sems):
    @pl.when(edge_ref[0] == 1)
    def _():
        fetch = pltpu.make_async_copy(fixed_ref, rows_ref, sems.at[0])
        fetch.start()
        fetch.wait()

    @pl.when(edge_ref[0] == 0)
    def _():
        rows_ref[...] = moved_ref[...]

    keep = pltpu.make_async_copy(rows_ref, hidden_ref, sems.at[1])
    keep.start()
    rows = rows_ref[...].astype(F32)
    inv = lax.rsqrt(jnp.mean(rows * rows, axis=-1, keepdims=True) + norm_eps)
    normed = (rows * inv * gain_ref[...]).astype(BF)
    mixed = jnp.dot(normed, w_ref[...], preferred_element_type=F32)
    for h in range(KV_HEADS):
        k = mixed[:, h * HEAD_DIM : (h + 1) * HEAD_DIM]
        turned = k * cos_ref[...] + pltpu.roll(k, HEAD_DIM // 2, 1) * sin_ref[...]
        out_ref[h, 0] = turned.astype(BF)
        v = (KV_HEADS + h) * HEAD_DIM
        out_ref[h, 1] = mixed[:, v : v + HEAD_DIM].astype(BF)
    keep.wait()


def project(edge, moved, fixed, gain, weight, cosine, sine):
    return pl.pallas_call(
        project_body,
        out_shape=[
            jax.ShapeDtypeStruct((KV_HEADS, 2, BLOCK, HEAD_DIM), BF),
            jax.ShapeDtypeStruct((BLOCK, D), BF),
        ],
        in_specs=[smem(), vmem(), hbm(), vmem(), vmem(), vmem(), vmem()],
        out_specs=[vmem(), hbm()],
        scratch_shapes=[pltpu.VMEM((BLOCK, D), BF), pltpu.SemaphoreType.DMA((2,))],
        compiler_params=params(12),
    )(edge, moved, fixed, gain, weight, cosine, sine)


def attend_body(*refs):
    place_ref, valid_ref = refs[:2]
    qg_refs = refs[2:6]
    kv_refs = refs[6:15]
    out_refs = refs[15:19]
    d_refs = refs[19:28]
    qg_ref, out_ref, held, keys_ref, values_ref, total, total_b, sems = refs[28:]
    b = pl.program_id(0)

    half = NX // 2

    @pl.when(b == 0)
    def _():
        for r in range(4):
            held[r] = kv_refs[r][...]
        held[4, :half] = kv_refs[4][...]
        held[4, half:] = kv_refs[5][...]
        for r in range(5, NZ):
            held[r] = kv_refs[r + 1][...]
        for k in range(NX):
            qg_ref[k] = qg_refs[k][: 2 * HEAD_DIM, :]
        total[...] = jnp.zeros_like(total)

    for s in range(SLOTS):
        at = place_ref[b * SLOTS + s]
        keys_ref[s * BLOCK : (s + 1) * BLOCK, :] = held[at // NX, at % NX, 0]
        values_ref[s * BLOCK : (s + 1) * BLOCK, :] = held[at // NX, at % NX, 1]

    keys = keys_ref[...]
    values = values_ref[...]
    q_t = qg_ref[b, :HEAD_DIM, :]
    g_t = qg_ref[b, HEAD_DIM:, :]
    scores = jnp.dot(keys, q_t, preferred_element_type=F32) * (score_scale * log2e)
    key_row = lax.broadcasted_iota(jnp.int32, (BLOCK, WIDE), 0)
    query_row = lax.broadcasted_iota(jnp.int32, (BLOCK, WIDE), 1) % BLOCK
    parts = [jnp.where(key_row <= query_row, scores[:BLOCK], masked_score)]
    for s in range(1, SLOTS):
        bias = jnp.where(valid_ref[b * SLOTS + s] > 0, 0.0, masked_score).astype(F32)
        parts.append(scores[s * BLOCK : (s + 1) * BLOCK] + bias)
    scores = jnp.concatenate(parts, axis=0)
    highest = jnp.max(scores, axis=0, keepdims=True)
    weights = jnp.exp2(scores - highest)
    inv = 1.0 / jnp.sum(weights, axis=0, keepdims=True)
    weights_b = weights.astype(BF)
    over_rows = (((0,), (0,)), ((), ()))
    over_cols = (((1,), (1,)), ((), ()))
    out_t = lax.dot_general(values, weights_b, over_rows, preferred_element_type=F32) * inv
    out_ref[b, :HEAD_DIM] = out_t.astype(BF)
    g_scaled = (g_t.astype(F32) * inv).astype(BF)
    delta = jnp.sum(out_t * g_scaled.astype(F32), axis=0, keepdims=True)
    d_probs = jnp.dot(values, g_scaled, preferred_element_type=F32)
    d_scores = (weights * (d_probs - delta)).astype(BF)
    dq_t = lax.dot_general(keys, d_scores, over_rows, preferred_element_type=F32) * score_scale
    out_ref[b, HEAD_DIM:] = dq_t.astype(BF)
    d_values = lax.dot_general(weights_b, g_scaled, over_cols, preferred_element_type=F32)
    d_keys = lax.dot_general(d_scores, q_t, over_cols, preferred_element_type=F32) * score_scale
    for s in range(SLOTS):
        at = place_ref[b * SLOTS + s]
        total[at // NX, at % NX, 0] += d_keys[s * BLOCK : (s + 1) * BLOCK]
        total[at // NX, at % NX, 1] += d_values[s * BLOCK : (s + 1) * BLOCK]

    @pl.when(b == NX - 1)
    def _():
        copies = []
        for i, at in (
            (3, (3,)),
            (6, (5,)),
            (4, (4, slice(0, half))),
            (5, (4, slice(half, NX))),
            (2, (2,)),
            (7, (6,)),
            (1, (1,)),
            (8, (7,)),
            (0, (0,)),
        ):
            total_b[at] = total[at].astype(BF)
            copies.append(pltpu.make_async_copy(total_b.at[at], d_refs[i], sems.at[i]))
            copies[-1].start()
        for k in range(NX):
            out_refs[k][...] = out_ref[k]
        for c in copies:
            c.wait()


def attend(place, valid, qg_pieces, kv_pieces):
    piece = (NX, 2, BLOCK, HEAD_DIM)
    shapes = [p.shape for p in kv_pieces]
    return pl.pallas_call(
        attend_body,
        grid=(NX,),
        out_shape=[jax.ShapeDtypeStruct((2 * HEAD_DIM, WIDE), BF)] * NX
        + [jax.ShapeDtypeStruct(s, BF) for s in shapes],
        in_specs=[smem(), smem()] + [vmem()] * (NX + len(shapes)),
        out_specs=[vmem()] * NX + [hbm()] * len(shapes),
        scratch_shapes=[
            pltpu.VMEM((NX, 2 * HEAD_DIM, WIDE), BF),
            pltpu.VMEM((NX, 2 * HEAD_DIM, WIDE), BF),
            pltpu.VMEM((NZ,) + piece, BF),
            pltpu.VMEM((KEYS, HEAD_DIM), BF),
            pltpu.VMEM((KEYS, HEAD_DIM), BF),
            pltpu.VMEM((NZ,) + piece, F32),
            pltpu.VMEM((NZ,) + piece, BF),
            pltpu.SemaphoreType.DMA((NZ + 1,)),
        ],
        compiler_params=params(20),
    )(place, valid, *qg_pieces, *kv_pieces)


def rows_body(where_ref, hidden_ref, *refs):
    back_refs, layer_ref, query_ref = refs[:NX], refs[NX], refs[NX + 1]
    for k in range(NX):
        x = (where_ref[1] + k) % NX
        for g in range(GROUP):
            at = pl.ds(pl.multiple_of(x * WIDE + g * HEAD_DIM, HEAD_DIM), HEAD_DIM)
            lanes = slice(g * BLOCK, (g + 1) * BLOCK)
            rows = hidden_ref[:, at].astype(F32)
            layer_ref[:, at] = (rows + back_refs[k][:HEAD_DIM, lanes].T.astype(F32)).astype(BF)
            query_ref[:, at] = back_refs[k][HEAD_DIM:, lanes].T


def to_rows(where, hidden, back):
    return pl.pallas_call(
        rows_body,
        out_shape=[jax.ShapeDtypeStruct((BLOCK, D), BF)] * 2,
        in_specs=[smem()] + [vmem()] * (NX + 1),
        out_specs=[vmem(), vmem()],
        compiler_params=params(),
    )(where, hidden, *back)


def sum_body(*refs):
    total = refs[0][...].astype(F32)
    for r in refs[1:-1]:
        total = total + r[...].astype(F32)
    refs[-1][...] = total.astype(BF)


def sum_pieces(pieces):
    return pl.pallas_call(
        sum_body,
        out_shape=jax.ShapeDtypeStruct(pieces[0].shape, BF),
        in_specs=[vmem()] * len(pieces),
        out_specs=vmem(),
        compiler_params=params(),
    )(*pieces)


def join_body(up_own, up_far, up_half, down_own, down_far, down_half, up_out, down_out):
    half = NX // 2
    up_out[:half] = (
        up_own[:half].astype(F32) + up_far[:half].astype(F32) + up_half[...].astype(F32)
    ).astype(BF)
    up_out[half:] = (up_own[half:].astype(F32) + up_far[half:].astype(F32)).astype(BF)
    down_out[:half] = (down_own[:half].astype(F32) + down_far[:half].astype(F32)).astype(BF)
    down_out[half:] = (
        down_own[half:].astype(F32) + down_far[half:].astype(F32) + down_half[...].astype(F32)
    ).astype(BF)


def join_pieces(*pieces):
    return pl.pallas_call(
        join_body,
        out_shape=[jax.ShapeDtypeStruct(pieces[0].shape, BF)] * 2,
        in_specs=[vmem()] * 6,
        out_specs=[vmem(), vmem()],
        compiler_params=params(),
    )(*pieces)


def finish_body(hidden_ref, grads_ref, d_ref, gain_ref, w_ref, cos_ref, sin_ref, out_ref):
    columns = []
    for h in range(KV_HEADS):
        k = d_ref[h, 0].astype(F32)
        columns.append(
            (k * cos_ref[...] - pltpu.roll(k, HEAD_DIM // 2, 1) * sin_ref[...]).astype(BF)
        )
    for h in range(KV_HEADS):
        columns.append(d_ref[h, 1])
    grads_kv = jnp.concatenate(columns, axis=-1)
    normed = lax.dot_general(
        grads_kv, w_ref[0], (((1,), (1,)), ((), ())), preferred_element_type=F32
    )
    rows = hidden_ref[...].astype(F32)
    grads = grads_ref[...].astype(F32)
    inv = lax.rsqrt(jnp.mean(rows * rows, axis=-1, keepdims=True) + norm_eps)
    scaled = normed * gain_ref[...]
    correction = jnp.mean(scaled * rows, axis=-1, keepdims=True)
    out_ref[...] = (grads + inv * scaled - rows * (inv * inv * inv * correction)).astype(BF)


def finish(hidden, grads, d_own, gain, weight, cosine, sine):
    return pl.pallas_call(
        finish_body,
        out_shape=jax.ShapeDtypeStruct((BLOCK, D), BF),
        in_specs=[vmem()] * 7,
        out_specs=vmem(),
        compiler_params=params(12),
    )(hidden, grads, d_own, gain, weight, cosine, sine)


def per_device(
    carried_rows,
    fresh_rows,
    queries,
    next_grads,
    loss_grads,
    projection,
    norm_gain,
    key_blocks,
    key_valid,
):
    section_now = lax.axis_index("section")
    section_last = lax.axis_size("section") - 1
    me = lax.axis_index("ctx")
    my_z = me % NZ
    first = (section_now == 0).astype(jnp.int32).reshape(1)
    last = (section_now == section_last).astype(jnp.int32).reshape(1)
    weight, gain = stage(projection, norm_gain)
    cosine, sine = turn_tables(me)

    h_moved = shift_section(carried_rows[0], 1)
    g_moved = shift_section(next_grads[0], -1)

    lists = jnp.concatenate([key_blocks[0], key_valid[0]], axis=0).astype(BF)
    lists = jnp.pad(lists, ((0, LIST_ROWS - 2), (0, WIDE - SLOTS)))

    kv_split, hidden = project(first, h_moved, fresh_rows, gain, weight, cosine, sine)
    kv_own = swap_x(kv_split)
    half = NX // 2
    up, down = [kv_own], [kv_own]
    for _ in range(3):
        up.append(shift_z(up[-1], 1))
        down.append(shift_z(down[-1], -1))
    up4 = shift_z(up[3][:half], 1)
    down4 = shift_z(down[3][half:], -1)

    where = jnp.stack([last[0], me // NZ])
    *qg_split, grads = split_rows(where, queries[0], g_moved, loss_grads, lists)
    qg = [qg_split[0]] + [shift_x(qg_split[k], k) for k in range(1, NX)]
    named = jnp.stack([p[2 * HEAD_DIM, :SLOTS] for p in qg]).astype(jnp.int32)
    valid = jnp.stack([p[2 * HEAD_DIM + 1, :SLOTS] for p in qg]).astype(jnp.int32)
    place = ((my_z - named % NZ) % NZ) * NX + named // NZ
    pieces = [kv_own, up[1], up[2], up[3], up4, down4, down[3], down[2], down[1]]

    outs = attend(place.reshape(-1), valid.reshape(-1), qg, pieces)
    back, (d0, d1, d2, d3, d4_up, d4_down, d5, d6, d7) = outs[:NX], outs[NX:]
    back = [back[0]] + [shift_x(back[k], -k) for k in range(1, NX)]
    far_up = shift_z(d3, -1)
    far_down = shift_z(d5, 1)
    half_up = shift_z(d4_up, -2)
    half_down = shift_z(d4_down, 2)
    near_up = shift_z(d1, -1)
    near_down = shift_z(d7, 1)
    both_up, both_down = join_pieces(d2, far_up, half_up, d6, far_down, half_down)
    both_up = shift_z(both_up, -2)
    both_down = shift_z(both_down, 2)
    layer_out, query_gradient = to_rows(where, hidden, back)
    gathered = [d0, near_up, near_down, both_up, both_down]
    gathered, layer_out = lax.optimization_barrier((gathered, layer_out))
    d_own = swap_x(sum_pieces(gathered))
    input_grads = finish(
        hidden, grads, d_own, norm_gain, projection, cosine, sine
    )
    return layer_out[None], query_gradient[None], input_grads[None]


def solution(mesh):
    placed = (
        P("section", "ctx", None),
        P("ctx", None),
        P("section", "ctx", None),
        P("section", "ctx", None),
        P("ctx", None),
        P("section", None, None),
        P("section", None),
        P("section", "ctx", None),
        P("section", "ctx", None),
    )
    return jax.shard_map(
        per_device,
        mesh=mesh,
        in_specs=placed,
        out_specs=(P("section", "ctx", None), P("section", "ctx", None), P("section", "ctx", None)),
        check_vma=False,
    )
```

```python
import jax
import jax.numpy as jnp
from jax import lax
from jax.experimental import pallas as pl
from jax.experimental.pallas import tpu as pltpu
from jax.sharding import PartitionSpec as P

D = 2048
HEADS = 16
KV_HEADS = 4
HEAD_DIM = 128
BLOCK = 128
SLOTS = 8
GROUP = HEADS // KV_HEADS
WIDE = GROUP * HEAD_DIM
KEYS = SLOTS * BLOCK

NX = 4
NZ = 8
LIST_ROWS = 16
PER_STEP = 4
SKEW = 1
STAGE_PARTS = 8

rope_base = 500000.0
norm_eps = 1e-05
masked_score = -1e30
score_scale = HEAD_DIM ** (-0.5)
log2e = 1.4426950408889634

BF = jnp.bfloat16
F32 = jnp.float32


def shift_section(block, distance):
    devices = range(lax.axis_size("section"))
    route = [(i, i + distance) for i in devices if i + distance in devices]
    return lax.ppermute(block, "section", route)


def shift_z(block, distance):
    route = [
        (x * NZ + z, x * NZ + (z + distance) % NZ) for x in range(NX) for z in range(NZ)
    ]
    return lax.ppermute(block, "ctx", route)


def swap_x(pieces):
    groups = [[x * NZ + z for x in range(NX)] for z in range(NZ)]
    return lax.all_to_all(pieces, "ctx", 0, 0, axis_index_groups=groups)


def shift_x(block, distance):
    route = [
        (x * NZ + z, (x + distance) % NX * NZ + z) for x in range(NX) for z in range(NZ)
    ]
    return lax.ppermute(block, "ctx", route)


def vmem():
    return pl.BlockSpec(memory_space=pltpu.VMEM)


def smem():
    return pl.BlockSpec(memory_space=pltpu.SMEM)


def hbm():
    return pl.BlockSpec(memory_space=pltpu.HBM)


def params(mib=12):
    return pltpu.CompilerParams(vmem_limit_bytes=mib * 2**20)


def turn_tables(block):
    half = HEAD_DIM // 2
    freqs = rope_base ** (-(jnp.arange(half).astype(F32) * 2.0) / HEAD_DIM)
    positions = (block * BLOCK + jnp.arange(BLOCK, dtype=jnp.int32)).astype(F32)
    angles = positions[:, None] * freqs[None, :]
    cosine, sine = jnp.cos(angles), jnp.sin(angles)
    return jnp.concatenate([cosine, cosine], -1), jnp.concatenate([-sine, sine], -1)


def split_body(where_ref, q_ref, moved_ref, fixed_ref, list_ref, *refs):
    dest_refs, out_refs, grads_ref, sems = refs[: NX + 1], refs[NX + 1], refs[NX + 2], refs[NX + 3]

    @pl.when(where_ref[0] == 1)
    def _():
        fetch = pltpu.make_async_copy(fixed_ref, grads_ref, sems.at[0])
        fetch.start()
        fetch.wait()

    @pl.when(where_ref[0] == 0)
    def _():
        grads_ref[...] = moved_ref[...]

    copies = [pltpu.make_async_copy(grads_ref, dest_refs[NX], sems.at[NX])]
    copies[0].start()
    for k in (1, 2, 3, 0):
        x = (where_ref[1] + k) % NX
        for part, rows_ref in enumerate((q_ref, grads_ref)):
            first = part * HEAD_DIM
            for g in range(GROUP):
                at = pl.ds(pl.multiple_of(x * WIDE + g * HEAD_DIM, HEAD_DIM), HEAD_DIM)
                out_refs[k, first : first + HEAD_DIM, g * BLOCK : (g + 1) * BLOCK] = rows_ref[
                    :, at
                ].T
        out_refs[k, 2 * HEAD_DIM :, :] = list_ref[...]
        copies.append(pltpu.make_async_copy(out_refs.at[k], dest_refs[k], sems.at[k]))
        copies[-1].start()
    for c in copies:
        c.wait()


def split_rows(where, rows, moved, fixed, lists):
    return pl.pallas_call(
        split_body,
        out_shape=[jax.ShapeDtypeStruct((2 * HEAD_DIM + LIST_ROWS, WIDE), BF)] * NX
        + [jax.ShapeDtypeStruct((BLOCK, D), BF)],
        in_specs=[smem(), vmem(), vmem(), hbm(), vmem()],
        out_specs=[hbm()] * (NX + 1),
        scratch_shapes=[
            pltpu.VMEM((NX, 2 * HEAD_DIM + LIST_ROWS, WIDE), BF),
            pltpu.VMEM((BLOCK, D), BF),
            pltpu.SemaphoreType.DMA((NX + 1,)),
        ],
        compiler_params=params(),
    )(where, rows, moved, fixed, lists)


def stage_body(w_ref, gain_ref, w_out, gain_out, sems):
    part = D // STAGE_PARTS
    copies = [
        pltpu.make_async_copy(
            w_ref.at[0, p * part : (p + 1) * part, :],
            w_out.at[p * part : (p + 1) * part, :],
            sems.at[p],
        )
        for p in range(STAGE_PARTS)
    ]
    copies.append(pltpu.make_async_copy(gain_ref, gain_out, sems.at[STAGE_PARTS]))
    for c in copies:
        c.start()
    for c in copies:
        c.wait()


def stage(weight, gain):
    return pl.pallas_call(
        stage_body,
        out_shape=[
            jax.ShapeDtypeStruct(weight.shape[1:], BF),
            jax.ShapeDtypeStruct(gain.shape, F32),
        ],
        in_specs=[hbm(), hbm()],
        out_specs=[vmem(), vmem()],
        scratch_shapes=[pltpu.SemaphoreType.DMA((STAGE_PARTS + 1,))],
        compiler_params=params(8),
    )(weight, gain)


def project_body(edge_ref, moved_ref, fixed_ref, gain_ref, w_ref, cos_ref, sin_ref, out_ref, hidden_ref, rows_ref, sems):
    @pl.when(edge_ref[0] == 1)
    def _():
        fetch = pltpu.make_async_copy(fixed_ref, rows_ref, sems.at[0])
        fetch.start()
        fetch.wait()

    @pl.when(edge_ref[0] == 0)
    def _():
        rows_ref[...] = moved_ref[...]

    keep = pltpu.make_async_copy(rows_ref, hidden_ref, sems.at[1])
    keep.start()
    rows = rows_ref[...].astype(F32)
    inv = lax.rsqrt(jnp.mean(rows * rows, axis=-1, keepdims=True) + norm_eps)
    normed = (rows * inv * gain_ref[...]).astype(BF)
    mixed = jnp.dot(normed, w_ref[...], preferred_element_type=F32)
    for h in range(KV_HEADS):
        k = mixed[:, h * HEAD_DIM : (h + 1) * HEAD_DIM]
        turned = k * cos_ref[...] + pltpu.roll(k, HEAD_DIM // 2, 1) * sin_ref[...]
        out_ref[h, 0] = turned.astype(BF)
        v = (KV_HEADS + h) * HEAD_DIM
        out_ref[h, 1] = mixed[:, v : v + HEAD_DIM].astype(BF)
    keep.wait()


def project(edge, moved, fixed, gain, weight, cosine, sine):
    return pl.pallas_call(
        project_body,
        out_shape=[
            jax.ShapeDtypeStruct((KV_HEADS, 2, BLOCK, HEAD_DIM), BF),
            jax.ShapeDtypeStruct((BLOCK, D), BF),
        ],
        in_specs=[smem(), vmem(), hbm(), vmem(), vmem(), vmem(), vmem()],
        out_specs=[vmem(), hbm()],
        scratch_shapes=[pltpu.VMEM((BLOCK, D), BF), pltpu.SemaphoreType.DMA((2,))],
        compiler_params=params(12),
    )(edge, moved, fixed, gain, weight, cosine, sine)


def attend_body(*refs):
    place_ref, valid_ref = refs[:2]
    qg_refs = refs[2:6]
    kv_refs = refs[6:15]
    out_refs = refs[15:19]
    d_refs = refs[19:28]
    held, keys_ref, values_ref, total, scores_ref, weights_ref, d_scores_ref = refs[28:]
    b = pl.program_id(0)

    half = NX // 2

    @pl.when(b == 0)
    def _():
        for r in range(4):
            held[r] = kv_refs[r][...]
        held[4, :half] = kv_refs[4][...]
        held[4, half:] = kv_refs[5][...]
        for r in range(5, NZ):
            held[r] = kv_refs[r + 1][...]
        total[...] = jnp.zeros_like(total)

    scale = score_scale * log2e
    over_rows = (((0,), (0,)), ((), ()))
    over_cols = (((1,), (1,)), ((), ()))
    fold = lambda x, op: op(x.reshape(BLOCK // 8, 8, WIDE), axis=0)
    key_row = lax.broadcasted_iota(jnp.int32, (BLOCK, WIDE), 0)
    query_row = lax.broadcasted_iota(jnp.int32, (BLOCK, WIDE), 1) % BLOCK
    tiles = [slice(s * BLOCK, (s + 1) * BLOCK) for s in range(SLOTS)]

    def phases(n):
        i = b * PER_STEP + n
        keys_n, values_n = keys_ref.at[n], values_ref.at[n]
        scores_n, weights_n, d_scores_n = scores_ref.at[n], weights_ref.at[n], d_scores_ref.at[n]
        for s in range(SLOTS):
            at = place_ref[i * SLOTS + s]
            keys_n[tiles[s], :] = held[at // NX, at % NX, 0]
            values_n[tiles[s], :] = held[at // NX, at % NX, 1]
        q_t = qg_refs[n][:HEAD_DIM, :]
        g_t = qg_refs[n][HEAD_DIM : 2 * HEAD_DIM, :]
        top = None
        for s in range(SLOTS):
            part = jnp.dot(keys_n[tiles[s], :], q_t, preferred_element_type=F32)
            if s == 0:
                part = jnp.where(key_row <= query_row, part, masked_score)
            else:
                part = part + jnp.where(valid_ref[i * SLOTS + s] > 0, 0.0, masked_score).astype(F32)
            scores_n[tiles[s], :] = part
            best = fold(part, jnp.max)
            top = best if top is None else jnp.maximum(top, best)
        yield
        highest = jnp.max(top, axis=0, keepdims=True) * scale
        count = None
        for s in range(SLOTS):
            part = jnp.exp2(scores_n[tiles[s], :] * scale - highest)
            weights_n[tiles[s], :] = part.astype(BF)
            some = fold(part, jnp.sum)
            count = some if count is None else count + some
        inv = 1.0 / jnp.sum(count, axis=0, keepdims=True)
        yield
        out_t = (
            lax.dot_general(values_n[...], weights_n[...], over_rows, preferred_element_type=F32)
            * inv
        )
        out_refs[n][:HEAD_DIM, :] = out_t.astype(BF)
        g_scaled = (g_t.astype(F32) * inv).astype(BF)
        delta = jnp.sum(out_t * g_scaled.astype(F32), axis=0, keepdims=True)
        d_values = lax.dot_general(weights_n[...], g_scaled, over_cols, preferred_element_type=F32)
        for s in range(SLOTS):
            at = place_ref[i * SLOTS + s]
            total[at // NX, at % NX, 1] += d_values[tiles[s]]
        yield
        for s in range(SLOTS):
            part = jnp.dot(values_n[tiles[s], :], g_scaled, preferred_element_type=F32)
            d_scores_n[tiles[s], :] = (weights_n[tiles[s], :].astype(F32) * (part - delta)).astype(BF)
        yield
        d_scores = d_scores_n[...]
        dq_t = (
            lax.dot_general(keys_n[...], d_scores, over_rows, preferred_element_type=F32)
            * score_scale
        )
        out_refs[n][HEAD_DIM:, :] = dq_t.astype(BF)
        d_keys = lax.dot_general(d_scores, q_t, over_cols, preferred_element_type=F32) * score_scale
        for s in range(SLOTS):
            at = place_ref[i * SLOTS + s]
            total[at // NX, at % NX, 0] += d_keys[tiles[s]]
        yield

    works = [phases(n) for n in range(PER_STEP)]
    if SKEW:
        for t in range(5 + PER_STEP - 1):
            for n, work in enumerate(works):
                if 0 <= t - n < 5:
                    next(work)
    else:
        for t in range(5):
            for work in works:
                next(work)

    @pl.when(b == NX // PER_STEP - 1)
    def _():
        for r in range(4):
            d_refs[r][...] = total[r].astype(BF)
        d_refs[4][...] = total[4, :half].astype(BF)
        d_refs[5][...] = total[4, half:].astype(BF)
        for r in range(5, NZ):
            d_refs[r + 1][...] = total[r].astype(BF)


def attend(place, valid, qg_pieces, kv_pieces):
    piece = (NX, 2, BLOCK, HEAD_DIM)
    shapes = [p.shape for p in kv_pieces]
    return pl.pallas_call(
        attend_body,
        grid=(NX // PER_STEP,),
        out_shape=[jax.ShapeDtypeStruct((2 * HEAD_DIM, WIDE), BF)] * NX
        + [jax.ShapeDtypeStruct(s, BF) for s in shapes],
        in_specs=[smem(), smem()] + [vmem()] * (NX + len(shapes)),
        out_specs=[vmem()] * (NX + len(shapes)),
        scratch_shapes=[
            pltpu.VMEM((NZ,) + piece, BF),
            pltpu.VMEM((PER_STEP, KEYS, HEAD_DIM), BF),
            pltpu.VMEM((PER_STEP, KEYS, HEAD_DIM), BF),
            pltpu.VMEM((NZ,) + piece, F32),
            pltpu.VMEM((PER_STEP, KEYS, WIDE), F32),
            pltpu.VMEM((PER_STEP, KEYS, WIDE), BF),
            pltpu.VMEM((PER_STEP, KEYS, WIDE), BF),
        ],
        compiler_params=params(30),
    )(place, valid, *qg_pieces, *kv_pieces)


def rows_body(where_ref, hidden_ref, *refs):
    back_refs, layer_ref, query_ref = refs[:NX], refs[NX], refs[NX + 1]
    for k in range(NX):
        x = (where_ref[1] + k) % NX
        for g in range(GROUP):
            at = pl.ds(pl.multiple_of(x * WIDE + g * HEAD_DIM, HEAD_DIM), HEAD_DIM)
            lanes = slice(g * BLOCK, (g + 1) * BLOCK)
            rows = hidden_ref[:, at].astype(F32)
            layer_ref[:, at] = (rows + back_refs[k][:HEAD_DIM, lanes].T.astype(F32)).astype(BF)
            query_ref[:, at] = back_refs[k][HEAD_DIM:, lanes].T


def to_rows(where, hidden, back):
    return pl.pallas_call(
        rows_body,
        out_shape=[jax.ShapeDtypeStruct((BLOCK, D), BF)] * 2,
        in_specs=[smem()] + [vmem()] * (NX + 1),
        out_specs=[vmem(), vmem()],
        compiler_params=params(),
    )(where, hidden, *back)


def sum_body(*refs):
    total = refs[0][...].astype(F32)
    for r in refs[1:-1]:
        total = total + r[...].astype(F32)
    refs[-1][...] = total.astype(BF)


def sum_pieces(pieces):
    return pl.pallas_call(
        sum_body,
        out_shape=jax.ShapeDtypeStruct(pieces[0].shape, BF),
        in_specs=[vmem()] * len(pieces),
        out_specs=vmem(),
        compiler_params=params(),
    )(*pieces)


def join_body(up_own, up_far, up_half, down_own, down_far, down_half, up_out, down_out):
    half = NX // 2
    up_out[:half] = (
        up_own[:half].astype(F32) + up_far[:half].astype(F32) + up_half[...].astype(F32)
    ).astype(BF)
    up_out[half:] = (up_own[half:].astype(F32) + up_far[half:].astype(F32)).astype(BF)
    down_out[:half] = (down_own[:half].astype(F32) + down_far[:half].astype(F32)).astype(BF)
    down_out[half:] = (
        down_own[half:].astype(F32) + down_far[half:].astype(F32) + down_half[...].astype(F32)
    ).astype(BF)


def join_pieces(*pieces):
    return pl.pallas_call(
        join_body,
        out_shape=[jax.ShapeDtypeStruct(pieces[0].shape, BF)] * 2,
        in_specs=[vmem()] * 6,
        out_specs=[vmem(), vmem()],
        compiler_params=params(),
    )(*pieces)


def finish_body(hidden_ref, grads_ref, d_ref, gain_ref, w_ref, cos_ref, sin_ref, out_ref):
    columns = []
    for h in range(KV_HEADS):
        k = d_ref[h, 0].astype(F32)
        columns.append(
            (k * cos_ref[...] - pltpu.roll(k, HEAD_DIM // 2, 1) * sin_ref[...]).astype(BF)
        )
    for h in range(KV_HEADS):
        columns.append(d_ref[h, 1])
    grads_kv = jnp.concatenate(columns, axis=-1)
    normed = lax.dot_general(
        grads_kv, w_ref[0], (((1,), (1,)), ((), ())), preferred_element_type=F32
    )
    rows = hidden_ref[...].astype(F32)
    grads = grads_ref[...].astype(F32)
    inv = lax.rsqrt(jnp.mean(rows * rows, axis=-1, keepdims=True) + norm_eps)
    scaled = normed * gain_ref[...]
    correction = jnp.mean(scaled * rows, axis=-1, keepdims=True)
    out_ref[...] = (grads + inv * scaled - rows * (inv * inv * inv * correction)).astype(BF)


def finish(hidden, grads, d_own, gain, weight, cosine, sine):
    return pl.pallas_call(
        finish_body,
        out_shape=jax.ShapeDtypeStruct((BLOCK, D), BF),
        in_specs=[vmem()] * 7,
        out_specs=vmem(),
        compiler_params=params(12),
    )(hidden, grads, d_own, gain, weight, cosine, sine)


def per_device(
    carried_rows,
    fresh_rows,
    queries,
    next_grads,
    loss_grads,
    projection,
    norm_gain,
    key_blocks,
    key_valid,
):
    section_now = lax.axis_index("section")
    section_last = lax.axis_size("section") - 1
    me = lax.axis_index("ctx")
    my_z = me % NZ
    first = (section_now == 0).astype(jnp.int32).reshape(1)
    last = (section_now == section_last).astype(jnp.int32).reshape(1)
    weight, gain = stage(projection, norm_gain)
    cosine, sine = turn_tables(me)

    h_moved = shift_section(carried_rows[0], 1)
    g_moved = shift_section(next_grads[0], -1)

    lists = jnp.concatenate([key_blocks[0], key_valid[0]], axis=0).astype(BF)
    lists = jnp.pad(lists, ((0, LIST_ROWS - 2), (0, WIDE - SLOTS)))

    kv_split, hidden = project(first, h_moved, fresh_rows, gain, weight, cosine, sine)
    kv_own = swap_x(kv_split)
    half = NX // 2
    up, down = [kv_own], [kv_own]
    for _ in range(3):
        up.append(shift_z(up[-1], 1))
        down.append(shift_z(down[-1], -1))
    up4 = shift_z(up[3][:half], 1)
    down4 = shift_z(down[3][half:], -1)

    where = jnp.stack([last[0], me // NZ])
    *qg_split, grads = split_rows(where, queries[0], g_moved, loss_grads, lists)
    qg = [qg_split[0]] + [shift_x(qg_split[k], k) for k in range(1, NX)]
    named = jnp.stack([p[2 * HEAD_DIM, :SLOTS] for p in qg]).astype(jnp.int32)
    valid = jnp.stack([p[2 * HEAD_DIM + 1, :SLOTS] for p in qg]).astype(jnp.int32)
    place = ((my_z - named % NZ) % NZ) * NX + named // NZ
    pieces = [kv_own, up[1], up[2], up[3], up4, down4, down[3], down[2], down[1]]

    outs = attend(place.reshape(-1), valid.reshape(-1), qg, pieces)
    back, (d0, d1, d2, d3, d4_up, d4_down, d5, d6, d7) = outs[:NX], outs[NX:]
    far_up = shift_z(d3, -1)
    far_down = shift_z(d5, 1)
    half_up = shift_z(d4_up, -2)
    half_down = shift_z(d4_down, 2)
    back, half_up, half_down = lax.optimization_barrier((back, half_up, half_down))
    back = [back[0]] + [shift_x(back[k], -k) for k in range(1, NX)]
    near_up = shift_z(d1, -1)
    near_down = shift_z(d7, 1)
    both_up, both_down = join_pieces(d2, far_up, half_up, d6, far_down, half_down)
    both_up = shift_z(both_up, -2)
    both_down = shift_z(both_down, 2)
    layer_out, query_gradient = to_rows(where, hidden, back)
    gathered = [d0, near_up, near_down, both_up, both_down]
    gathered, layer_out = lax.optimization_barrier((gathered, layer_out))
    d_own = swap_x(sum_pieces(gathered))
    input_grads = finish(
        hidden, grads, d_own, norm_gain, projection, cosine, sine
    )
    return layer_out[None], query_gradient[None], input_grads[None]


def solution(mesh):
    placed = (
        P("section", "ctx", None),
        P("ctx", None),
        P("section", "ctx", None),
        P("section", "ctx", None),
        P("ctx", None),
        P("section", None, None),
        P("section", None),
        P("section", "ctx", None),
        P("section", "ctx", None),
    )
    return jax.shard_map(
        per_device,
        mesh=mesh,
        in_specs=placed,
        out_specs=(P("section", "ctx", None), P("section", "ctx", None), P("section", "ctx", None)),
        check_vma=False,
    )
```

```python
import jax
import jax.numpy as jnp
from jax import lax
from jax.experimental import pallas as pl
from jax.experimental.pallas import tpu as pltpu
from jax.sharding import PartitionSpec as P

D = 2048
HEADS = 16
KV_HEADS = 4
HEAD_DIM = 128
BLOCK = 128
SLOTS = 8
GROUP = HEADS // KV_HEADS
WIDE = GROUP * HEAD_DIM
KEYS = SLOTS * BLOCK

NX = 4
NZ = 8
LIST_ROWS = 16
PER_STEP = 4
SKEW = 1
STAGE_PARTS = 8

rope_base = 500000.0
norm_eps = 1e-05
masked_score = -1e30
score_scale = HEAD_DIM ** (-0.5)
log2e = 1.4426950408889634

BF = jnp.bfloat16
F32 = jnp.float32


def shift_section(block, distance):
    devices = range(lax.axis_size("section"))
    route = [(i, i + distance) for i in devices if i + distance in devices]
    return lax.ppermute(block, "section", route)


def shift_z(block, distance):
    route = [
        (x * NZ + z, x * NZ + (z + distance) % NZ) for x in range(NX) for z in range(NZ)
    ]
    return lax.ppermute(block, "ctx", route)


def swap_x(pieces):
    groups = [[x * NZ + z for x in range(NX)] for z in range(NZ)]
    return lax.all_to_all(pieces, "ctx", 0, 0, axis_index_groups=groups)


def shift_x(block, distance):
    route = [
        (x * NZ + z, (x + distance) % NX * NZ + z) for x in range(NX) for z in range(NZ)
    ]
    return lax.ppermute(block, "ctx", route)


def vmem():
    return pl.BlockSpec(memory_space=pltpu.VMEM)


def smem():
    return pl.BlockSpec(memory_space=pltpu.SMEM)


def hbm():
    return pl.BlockSpec(memory_space=pltpu.HBM)


def params(mib=12):
    return pltpu.CompilerParams(vmem_limit_bytes=mib * 2**20)


def turn_tables(block):
    half = HEAD_DIM // 2
    freqs = rope_base ** (-(jnp.arange(half).astype(F32) * 2.0) / HEAD_DIM)
    positions = (block * BLOCK + jnp.arange(BLOCK, dtype=jnp.int32)).astype(F32)
    angles = positions[:, None] * freqs[None, :]
    cosine, sine = jnp.cos(angles), jnp.sin(angles)
    return jnp.concatenate([cosine, cosine], -1), jnp.concatenate([-sine, sine], -1)


def split_body(where_ref, q_ref, moved_ref, fixed_ref, list_ref, *refs):
    dest_refs, out_refs, grads_ref, sems = refs[: NX + 1], refs[NX + 1], refs[NX + 2], refs[NX + 3]

    @pl.when(where_ref[0] == 1)
    def _():
        fetch = pltpu.make_async_copy(fixed_ref, grads_ref, sems.at[0])
        fetch.start()
        fetch.wait()

    @pl.when(where_ref[0] == 0)
    def _():
        grads_ref[...] = moved_ref[...]

    copies = [pltpu.make_async_copy(grads_ref, dest_refs[NX], sems.at[NX])]
    copies[0].start()
    for k in (1, 2, 3, 0):
        x = (where_ref[1] + k) % NX
        for part, rows_ref in enumerate((q_ref, grads_ref)):
            first = part * HEAD_DIM
            for g in range(GROUP):
                at = pl.ds(pl.multiple_of(x * WIDE + g * HEAD_DIM, HEAD_DIM), HEAD_DIM)
                out_refs[k, first : first + HEAD_DIM, g * BLOCK : (g + 1) * BLOCK] = rows_ref[
                    :, at
                ].T
        out_refs[k, 2 * HEAD_DIM :, :] = list_ref[...]
        copies.append(pltpu.make_async_copy(out_refs.at[k], dest_refs[k], sems.at[k]))
        copies[-1].start()
    for c in copies:
        c.wait()


def split_rows(where, rows, moved, fixed, lists):
    return pl.pallas_call(
        split_body,
        out_shape=[jax.ShapeDtypeStruct((2 * HEAD_DIM + LIST_ROWS, WIDE), BF)] * NX
        + [jax.ShapeDtypeStruct((BLOCK, D), BF)],
        in_specs=[smem(), vmem(), vmem(), hbm(), vmem()],
        out_specs=[hbm()] * (NX + 1),
        scratch_shapes=[
            pltpu.VMEM((NX, 2 * HEAD_DIM + LIST_ROWS, WIDE), BF),
            pltpu.VMEM((BLOCK, D), BF),
            pltpu.SemaphoreType.DMA((NX + 1,)),
        ],
        compiler_params=params(),
    )(where, rows, moved, fixed, lists)


def stage_body(w_ref, gain_ref, w_out, gain_out, sems):
    part = D // STAGE_PARTS
    copies = [
        pltpu.make_async_copy(
            w_ref.at[0, p * part : (p + 1) * part, :],
            w_out.at[p * part : (p + 1) * part, :],
            sems.at[p],
        )
        for p in range(STAGE_PARTS)
    ]
    copies.append(pltpu.make_async_copy(gain_ref, gain_out, sems.at[STAGE_PARTS]))
    for c in copies:
        c.start()
    for c in copies:
        c.wait()


def stage(weight, gain):
    return pl.pallas_call(
        stage_body,
        out_shape=[
            jax.ShapeDtypeStruct(weight.shape[1:], BF),
            jax.ShapeDtypeStruct(gain.shape, F32),
        ],
        in_specs=[hbm(), hbm()],
        out_specs=[vmem(), vmem()],
        scratch_shapes=[pltpu.SemaphoreType.DMA((STAGE_PARTS + 1,))],
        compiler_params=params(8),
    )(weight, gain)


def project_body(edge_ref, moved_ref, fixed_ref, gain_ref, w_ref, cos_ref, sin_ref, out_ref, hidden_ref, rows_ref, sems):
    @pl.when(edge_ref[0] == 1)
    def _():
        fetch = pltpu.make_async_copy(fixed_ref, rows_ref, sems.at[0])
        fetch.start()
        fetch.wait()

    @pl.when(edge_ref[0] == 0)
    def _():
        rows_ref[...] = moved_ref[...]

    keep = pltpu.make_async_copy(rows_ref, hidden_ref, sems.at[1])
    keep.start()
    rows = rows_ref[...].astype(F32)
    inv = lax.rsqrt(jnp.mean(rows * rows, axis=-1, keepdims=True) + norm_eps)
    normed = (rows * inv * gain_ref[...]).astype(BF)
    mixed = jnp.dot(normed, w_ref[...], preferred_element_type=F32)
    for h in range(KV_HEADS):
        k = mixed[:, h * HEAD_DIM : (h + 1) * HEAD_DIM]
        turned = k * cos_ref[...] + pltpu.roll(k, HEAD_DIM // 2, 1) * sin_ref[...]
        out_ref[h, 0] = turned.astype(BF)
        v = (KV_HEADS + h) * HEAD_DIM
        out_ref[h, 1] = mixed[:, v : v + HEAD_DIM].astype(BF)
    keep.wait()


def project(edge, moved, fixed, gain, weight, cosine, sine):
    return pl.pallas_call(
        project_body,
        out_shape=[
            jax.ShapeDtypeStruct((KV_HEADS, 2, BLOCK, HEAD_DIM), BF),
            jax.ShapeDtypeStruct((BLOCK, D), BF),
        ],
        in_specs=[smem(), vmem(), hbm(), vmem(), vmem(), vmem(), vmem()],
        out_specs=[vmem(), hbm()],
        scratch_shapes=[pltpu.VMEM((BLOCK, D), BF), pltpu.SemaphoreType.DMA((2,))],
        compiler_params=params(12),
    )(edge, moved, fixed, gain, weight, cosine, sine)


def attend_body(*refs):
    place_ref, valid_ref = refs[:2]
    qg_refs = refs[2:6]
    kv_refs = refs[6:15]
    out_refs = refs[15:19]
    d_refs = refs[19:28]
    held, keys_ref, values_ref, total, scores_ref, weights_ref = refs[28:]
    b = pl.program_id(0)

    half = NX // 2

    @pl.when(b == 0)
    def _():
        for r in range(4):
            held[r] = kv_refs[r][...]
        held[4, :half] = kv_refs[4][...]
        held[4, half:] = kv_refs[5][...]
        for r in range(5, NZ):
            held[r] = kv_refs[r + 1][...]
        total[...] = jnp.zeros_like(total)

    scale = score_scale * log2e
    over_rows = (((0,), (0,)), ((), ()))
    over_cols = (((1,), (1,)), ((), ()))
    fold = lambda x, op: op(x.reshape(BLOCK // 8, 8, WIDE), axis=0)
    key_row = lax.broadcasted_iota(jnp.int32, (BLOCK, WIDE), 0)
    query_row = lax.broadcasted_iota(jnp.int32, (BLOCK, WIDE), 1) % BLOCK
    tiles = [slice(s * BLOCK, (s + 1) * BLOCK) for s in range(SLOTS)]

    def phases(n):
        i = b * PER_STEP + n
        keys_n, values_n = keys_ref.at[n], values_ref.at[n]
        scores_n, weights_n = scores_ref.at[n], weights_ref.at[n]
        for s in range(SLOTS):
            at = place_ref[i * SLOTS + s]
            keys_n[tiles[s], :] = held[at // NX, at % NX, 0]
            values_n[tiles[s], :] = held[at // NX, at % NX, 1]
        q_t = qg_refs[n][:HEAD_DIM, :]
        g_t = qg_refs[n][HEAD_DIM : 2 * HEAD_DIM, :]
        top = None
        for s in range(SLOTS):
            part = jnp.dot(keys_n[tiles[s], :], q_t, preferred_element_type=F32)
            if s == 0:
                part = jnp.where(key_row <= query_row, part, masked_score)
            else:
                part = part + jnp.where(valid_ref[i * SLOTS + s] > 0, 0.0, masked_score).astype(F32)
            scores_n[tiles[s], :] = part
            best = fold(part, jnp.max)
            top = best if top is None else jnp.maximum(top, best)
        yield
        highest = jnp.max(top, axis=0, keepdims=True) * scale
        count = None
        for s in range(SLOTS):
            part = jnp.exp2(scores_n[tiles[s], :] * scale - highest)
            weights_n[tiles[s], :] = part.astype(BF)
            some = fold(part, jnp.sum)
            count = some if count is None else count + some
        inv = 1.0 / jnp.sum(count, axis=0, keepdims=True)
        yield
        out_t = (
            lax.dot_general(values_n[...], weights_n[...], over_rows, preferred_element_type=F32)
            * inv
        )
        out_refs[n][:HEAD_DIM, :] = out_t.astype(BF)
        g_scaled = (g_t.astype(F32) * inv).astype(BF)
        delta = jnp.sum(out_t * g_scaled.astype(F32), axis=0, keepdims=True)
        d_values = lax.dot_general(weights_n[...], g_scaled, over_cols, preferred_element_type=F32)
        for s in range(SLOTS):
            at = place_ref[i * SLOTS + s]
            total[at // NX, at % NX, 1] += d_values[tiles[s]]
        yield
        for s in range(SLOTS):
            part = jnp.dot(values_n[tiles[s], :], g_scaled, preferred_element_type=F32)
            weights_n[tiles[s], :] = (weights_n[tiles[s], :].astype(F32) * (part - delta)).astype(BF)
        yield
        d_scores = weights_n[...]
        dq_t = (
            lax.dot_general(keys_n[...], d_scores, over_rows, preferred_element_type=F32)
            * score_scale
        )
        out_refs[n][HEAD_DIM:, :] = dq_t.astype(BF)
        d_keys = lax.dot_general(d_scores, q_t, over_cols, preferred_element_type=F32) * score_scale
        for s in range(SLOTS):
            at = place_ref[i * SLOTS + s]
            total[at // NX, at % NX, 0] += d_keys[tiles[s]]
        yield

    works = [phases(n) for n in range(PER_STEP)]
    if SKEW:
        for t in range(5 + PER_STEP - 1):
            for n, work in enumerate(works):
                if 0 <= t - n < 5:
                    next(work)
    else:
        for t in range(5):
            for work in works:
                next(work)

    @pl.when(b == NX // PER_STEP - 1)
    def _():
        for r in range(4):
            d_refs[r][...] = total[r].astype(BF)
        d_refs[4][...] = total[4, :half].astype(BF)
        d_refs[5][...] = total[4, half:].astype(BF)
        for r in range(5, NZ):
            d_refs[r + 1][...] = total[r].astype(BF)


def attend(place, valid, qg_pieces, kv_pieces):
    piece = (NX, 2, BLOCK, HEAD_DIM)
    shapes = [p.shape for p in kv_pieces]
    return pl.pallas_call(
        attend_body,
        grid=(NX // PER_STEP,),
        out_shape=[jax.ShapeDtypeStruct((2 * HEAD_DIM, WIDE), BF)] * NX
        + [jax.ShapeDtypeStruct(s, BF) for s in shapes],
        in_specs=[smem(), smem()] + [vmem()] * (NX + len(shapes)),
        out_specs=[vmem()] * (NX + len(shapes)),
        scratch_shapes=[
            pltpu.VMEM((NZ,) + piece, BF),
            pltpu.VMEM((PER_STEP, KEYS, HEAD_DIM), BF),
            pltpu.VMEM((PER_STEP, KEYS, HEAD_DIM), BF),
            pltpu.VMEM((NZ,) + piece, F32),
            pltpu.VMEM((PER_STEP, KEYS, WIDE), F32),
            pltpu.VMEM((PER_STEP, KEYS, WIDE), BF),
        ],
        compiler_params=params(25),
    )(place, valid, *qg_pieces, *kv_pieces)


def rows_body(where_ref, hidden_ref, *refs):
    back_refs, layer_ref, query_ref = refs[:NX], refs[NX], refs[NX + 1]
    for k in range(NX):
        x = (where_ref[1] + k) % NX
        for g in range(GROUP):
            at = pl.ds(pl.multiple_of(x * WIDE + g * HEAD_DIM, HEAD_DIM), HEAD_DIM)
            lanes = slice(g * BLOCK, (g + 1) * BLOCK)
            rows = hidden_ref[:, at].astype(F32)
            layer_ref[:, at] = (rows + back_refs[k][:HEAD_DIM, lanes].T.astype(F32)).astype(BF)
            query_ref[:, at] = back_refs[k][HEAD_DIM:, lanes].T


def to_rows(where, hidden, back):
    return pl.pallas_call(
        rows_body,
        out_shape=[jax.ShapeDtypeStruct((BLOCK, D), BF)] * 2,
        in_specs=[smem()] + [vmem()] * (NX + 1),
        out_specs=[vmem(), vmem()],
        compiler_params=params(),
    )(where, hidden, *back)


def sum_body(where_ref, *refs):
    pieces, outs = refs[:-NX], refs[-NX:]
    for k in range(NX):
        x = (where_ref[1] + k) % NX
        total = pieces[0][x].astype(F32)
        for r in pieces[1:]:
            total = total + r[x].astype(F32)
        outs[k][...] = total.astype(BF)


def sum_pieces(where, pieces):
    return pl.pallas_call(
        sum_body,
        out_shape=[jax.ShapeDtypeStruct(pieces[0].shape[1:], BF)] * NX,
        in_specs=[smem()] + [vmem()] * len(pieces),
        out_specs=[vmem()] * NX,
        compiler_params=params(),
    )(where, *pieces)


def join_body(up_own, up_far, up_half, down_own, down_far, down_half, up_out, down_out):
    half = NX // 2
    up_out[:half] = (
        up_own[:half].astype(F32) + up_far[:half].astype(F32) + up_half[...].astype(F32)
    ).astype(BF)
    up_out[half:] = (up_own[half:].astype(F32) + up_far[half:].astype(F32)).astype(BF)
    down_out[:half] = (down_own[:half].astype(F32) + down_far[:half].astype(F32)).astype(BF)
    down_out[half:] = (
        down_own[half:].astype(F32) + down_far[half:].astype(F32) + down_half[...].astype(F32)
    ).astype(BF)


def join_pieces(*pieces):
    return pl.pallas_call(
        join_body,
        out_shape=[jax.ShapeDtypeStruct(pieces[0].shape, BF)] * 2,
        in_specs=[vmem()] * 6,
        out_specs=[vmem(), vmem()],
        compiler_params=params(),
    )(*pieces)


def finish_body(where_ref, hidden_ref, grads_ref, gain_ref, w_ref, cos_ref, sin_ref, *refs):
    d_refs, out_ref, columns_ref = refs[:NX], refs[NX], refs[NX + 1]
    for i in range(NX):
        h = (where_ref[1] + NX - i) % NX
        k = d_refs[i][0].astype(F32)
        at = pl.multiple_of(h * HEAD_DIM, HEAD_DIM)
        columns_ref[:, pl.ds(at, HEAD_DIM)] = (
            k * cos_ref[...] - pltpu.roll(k, HEAD_DIM // 2, 1) * sin_ref[...]
        ).astype(BF)
        at = pl.multiple_of((KV_HEADS + h) * HEAD_DIM, HEAD_DIM)
        columns_ref[:, pl.ds(at, HEAD_DIM)] = d_refs[i][1]
    grads_kv = columns_ref[...]
    normed = lax.dot_general(
        grads_kv, w_ref[0], (((1,), (1,)), ((), ())), preferred_element_type=F32
    )
    rows = hidden_ref[...].astype(F32)
    grads = grads_ref[...].astype(F32)
    inv = lax.rsqrt(jnp.mean(rows * rows, axis=-1, keepdims=True) + norm_eps)
    scaled = normed * gain_ref[...]
    correction = jnp.mean(scaled * rows, axis=-1, keepdims=True)
    out_ref[...] = (grads + inv * scaled - rows * (inv * inv * inv * correction)).astype(BF)


def finish(where, hidden, grads, d_own, gain, weight, cosine, sine):
    return pl.pallas_call(
        finish_body,
        out_shape=jax.ShapeDtypeStruct((BLOCK, D), BF),
        in_specs=[smem()] + [vmem()] * (6 + NX),
        out_specs=vmem(),
        scratch_shapes=[pltpu.VMEM((BLOCK, 2 * KV_HEADS * HEAD_DIM), BF)],
        compiler_params=params(12),
    )(where, hidden, grads, gain, weight, cosine, sine, *d_own)


def per_device(
    carried_rows,
    fresh_rows,
    queries,
    next_grads,
    loss_grads,
    projection,
    norm_gain,
    key_blocks,
    key_valid,
):
    section_now = lax.axis_index("section")
    section_last = lax.axis_size("section") - 1
    me = lax.axis_index("ctx")
    my_z = me % NZ
    first = (section_now == 0).astype(jnp.int32).reshape(1)
    last = (section_now == section_last).astype(jnp.int32).reshape(1)
    weight, gain = stage(projection, norm_gain)
    cosine, sine = turn_tables(me)

    h_moved = shift_section(carried_rows[0], 1)
    g_moved = shift_section(next_grads[0], -1)

    lists = jnp.concatenate([key_blocks[0], key_valid[0]], axis=0).astype(BF)
    lists = jnp.pad(lists, ((0, LIST_ROWS - 2), (0, WIDE - SLOTS)))

    kv_split, hidden = project(first, h_moved, fresh_rows, gain, weight, cosine, sine)
    kv_own = swap_x(kv_split)
    half = NX // 2
    up, down = [kv_own], [kv_own]
    for _ in range(3):
        up.append(shift_z(up[-1], 1))
        down.append(shift_z(down[-1], -1))
    up4 = shift_z(up[3][:half], 1)
    down4 = shift_z(down[3][half:], -1)

    where = jnp.stack([last[0], me // NZ])
    *qg_split, grads = split_rows(where, queries[0], g_moved, loss_grads, lists)
    (qg_split[2], qg_split[3]), up[1], down[1] = lax.optimization_barrier(
        ((qg_split[2], qg_split[3]), up[1], down[1])
    )
    qg = [qg_split[0]] + [shift_x(qg_split[k], k) for k in range(1, NX)]
    named = jnp.stack([p[2 * HEAD_DIM, :SLOTS] for p in qg]).astype(jnp.int32)
    valid = jnp.stack([p[2 * HEAD_DIM + 1, :SLOTS] for p in qg]).astype(jnp.int32)
    place = ((my_z - named % NZ) % NZ) * NX + named // NZ
    pieces = [kv_own, up[1], up[2], up[3], up4, down4, down[3], down[2], down[1]]

    outs = attend(place.reshape(-1), valid.reshape(-1), qg, pieces)
    back, (d0, d1, d2, d3, d4_up, d4_down, d5, d6, d7) = outs[:NX], outs[NX:]
    far_up = shift_z(d3, -1)
    far_down = shift_z(d5, 1)
    half_up = shift_z(d4_up, -2)
    half_down = shift_z(d4_down, 2)
    back, half_up, half_down = lax.optimization_barrier((back, half_up, half_down))
    back = [back[0]] + [shift_x(back[k], -k) for k in range(1, NX)]
    near_up = shift_z(d1, -1)
    near_down = shift_z(d7, 1)
    both_up, both_down = join_pieces(d2, far_up, half_up, d6, far_down, half_down)
    both_up = shift_z(both_up, -2)
    both_down = shift_z(both_down, 2)
    layer_out, query_gradient = to_rows(where, hidden, back)
    gathered = [d0, near_up, near_down, both_up, both_down]
    gathered, layer_out = lax.optimization_barrier((gathered, layer_out))
    sums = sum_pieces(where, gathered)
    d_own = [sums[0]] + [shift_x(sums[k], k) for k in range(1, NX)]
    input_grads = finish(
        where, hidden, grads, d_own, norm_gain, projection, cosine, sine
    )
    return layer_out[None], query_gradient[None], input_grads[None]


def solution(mesh):
    placed = (
        P("section", "ctx", None),
        P("ctx", None),
        P("section", "ctx", None),
        P("section", "ctx", None),
        P("ctx", None),
        P("section", None, None),
        P("section", None),
        P("section", "ctx", None),
        P("section", "ctx", None),
    )
    return jax.shard_map(
        per_device,
        mesh=mesh,
        in_specs=placed,
        out_specs=(P("section", "ctx", None), P("section", "ctx", None), P("section", "ctx", None)),
        check_vma=False,
    )
```
